32 devices in a mesh: section: 4 (over y, core), gy: 4 (over z), gx: 2 (over x).
Axes of the slice: x: 2, y: 2, z: 4, core: 2. Of those that a mesh axis runs over, the one named last changes fastest.
Arguments:
- fields: float32 [4, 15, 16, 32, 512], P('section', None, None, 'gy', 'gx'), may hold values from -2 to 2, as said below
- sea_mask: int32 [96, 512], replicated, may hold values 0 or 1
- bottom: int32 [96, 512], replicated, may hold values from 2 to 16
- reaction: float32 [15, 15], replicated, may hold values from -1.5 to 1.5
- growth: float32 [15], replicated, may hold values from 0.3 to 3
Outputs:
- advanced: float32 [4, 15, 16, 32, 512], P('section', None, None, 'gy', 'gx')
The draws below stay inside these ranges and needn't reach their ends.
Inputs may be any that keep to these rules, and one draw needn't show every extreme that they name: `fields`: in slab 0 the velocity channels lie within -1 to 1 and the turbulent energy channels within 0 to 1.5; tracer slabs are positive.
All inputs are finite; a program needn't handle non-finite values.
Results may differ from the reference program's by a relative error of at most 0.0003.
Values sent between devices are 32-bit elements; how exact they have to be, the bound alone decides.
A program may use at most 128 MiB of HBM per device.

```python
import math
import jax
import jax.numpy as jnp
from jax import lax

FIELDS = 5
TRACERS = 15
NZ = 16
TY = 8
STEPS = 2
ROWS = 32
NY = 96
NX = 512
N_GY = 4


def draw_fields(key, part):
    keys = jax.random.split(key, 4)
    extent = (3, NZ, ROWS, NX)
    velocity = jnp.clip(0.4 * jax.random.normal(keys[0], (6, NZ, ROWS, NX)), -1.0, 1.0)
    scalars = jnp.clip(jax.random.normal(keys[1], (6, NZ, ROWS, NX)), -2.0, 2.0)
    energy = 1.5 * jax.random.uniform(keys[2], extent)
    tracers = jax.random.uniform(keys[3], (3, TRACERS, NZ, ROWS, NX), minval=0.05, maxval=2.0)
    ocean_part = jnp.concatenate([velocity, scalars, energy], axis=0)
    return jnp.concatenate([ocean_part[None], tracers], axis=0).astype(jnp.float32)


def set_ends(drawn, own_key, smallest, top_value):
    index_at = [jax.random.randint(jax.random.fold_in(own_key, axis), (), 0, length) for axis, length in enumerate(drawn.shape)]
    widest = drawn.shape.index(max(drawn.shape))
    beside = index_at[:widest] + [(index_at[widest] + 1) % drawn.shape[widest]] + index_at[widest + 1:]
    return drawn.at[tuple(index_at)].set(smallest).at[tuple(beside)].set(top_value)


def scatter_about(key, shape, scale, reach, kind=jnp.bfloat16):
    result = scale * jax.random.normal(key, shape, jnp.float32)
    return jnp.clip(result, min=-reach, max=reach).astype(kind)


def setup_inputs(seed: int = 0) -> dict:
    key_list = jax.random.split(jax.random.key(seed), 6)
    fields = draw_fields(jax.random.fold_in(key_list[5], 71), 0)
    sea_mask = set_ends((jax.random.randint(key_list[1], (NY, NX), 0, 8) < 7).astype(jnp.int32), jax.random.fold_in(key_list[1], 1), 0, 1)
    bottom = set_ends(jax.random.randint(key_list[2], (NY, NX), 2, NZ + 1), jax.random.fold_in(key_list[2], 1), 2, NZ).astype(jnp.int32)
    reaction = scatter_about(key_list[3], (TRACERS, TRACERS), TRACERS ** -0.5, 1.5, jnp.float32)
    growth = jnp.clip(jnp.exp(jax.random.uniform(key_list[4], (TRACERS,), jnp.float32, math.log(0.3), math.log(3.0))), 0.3, 3.0)
    return {"fields": fields, "sea_mask": sea_mask, "bottom": bottom, "reaction": reaction, "growth": growth}


TIME_INCREMENT = 0.2
CORIOLIS = 0.5
PRESSURE = 0.5
VISCOSITY = 0.15
DRAG_RATE = 0.1
DIFFUSION_RATE = 0.15
THERMAL_FORCING = 3.0
SHEAR_GAIN = 0.5
DISSIPATION = 0.5
KAPPA_BASE = 0.05
KAPPA_GAIN = 0.15
EXPANSION = 0.2
CONTRACTION = 0.8
WATER_SHADE = 0.05
CHLOROPHYLL_SHADE = 0.1
HALF_SAT = 0.5


def limited(forward, backward):
    return 0.5 * (jnp.sign(forward) + jnp.sign(backward)) * jnp.minimum(jnp.abs(forward), jnp.abs(backward))


def face_flux(values, speeds, kappas, wetness, dimension):
    face_count = values.shape[dimension] - 3

    def window(source, offset):
        return lax.slice_in_dim(source, offset, offset + face_count, axis=dimension)

    before = window(values, 0)
    inside = window(values, 1)
    beyond = window(values, 2)
    farther = window(values, 3)
    opened = window(wetness, 1) * window(wetness, 2)
    speeds_open = window(speeds, 1) * opened
    upwind = inside + 0.5 * limited(beyond - inside, inside - before)
    downwind = beyond - 0.5 * limited(farther - beyond, beyond - inside)
    carried = jnp.maximum(speeds_open, 0.0) * upwind + jnp.minimum(speeds_open, 0.0) * downwind
    spread = 0.5 * (window(kappas, 1) + window(kappas, 2)) * (beyond - inside) * opened
    return carried - spread


def shading(tracers):
    chlorophyll = jnp.maximum(tracers[2], 0.0)
    absorbed = WATER_SHADE + CHLOROPHYLL_SHADE * chlorophyll
    optical = jnp.cumsum(absorbed, axis=0) - absorbed
    sunlight = jnp.exp(-optical)
    return sunlight, CHLOROPHYLL_SHADE * chlorophyll * sunlight


def tracer_update(padded, east_speed, north_speed, kappas, wetness, sunlight, reaction, growth):
    height = padded.shape[2] - 4
    breadth = padded.shape[3] - 4
    across = face_flux(padded[:, :, 2:height + 2, :], east_speed[:, :, 2:height + 2, :], kappas[:, :, 2:height + 2, :], wetness[:, :, 2:height + 2, :], 3)
    upward = face_flux(padded[:, :, :, 2:breadth + 2], north_speed[:, :, :, 2:breadth + 2], kappas[:, :, :, 2:breadth + 2], wetness[:, :, :, 2:breadth + 2], 2)
    tracers = padded[:, :, 2:height + 2, 2:breadth + 2]
    grid_point_is_wet = wetness[:, :, 2:height + 2, 2:breadth + 2]
    cell_kappa = kappas[:, :, 2:height + 2, 2:breadth + 2]
    horizontal = across[:, :, :, :-1] - across[:, :, :, 1:] + upward[:, :, :-1, :] - upward[:, :, 1:, :]
    level_open = grid_point_is_wet[:, 1:] * grid_point_is_wet[:, :-1]
    level_kappa = 0.5 * (cell_kappa[:, 1:] + cell_kappa[:, :-1])
    level_flux = level_kappa * (tracers[:, 1:] - tracers[:, :-1]) * level_open
    bounded = jnp.zeros_like(level_flux[:, :1])
    vertical = jnp.concatenate([level_flux, bounded], axis=1) - jnp.concatenate([bounded, level_flux], axis=1)
    nutrient = jnp.maximum(tracers[0], 0.0)
    uptake = nutrient / (nutrient + HALF_SAT) * sunlight
    growing = growth[:, None, None, None] * jnp.maximum(tracers, 0.0) * uptake[None]
    reacted = jnp.einsum('cd,dzyx->czyx', reaction, growing, precision=lax.Precision.HIGHEST)
    return grid_point_is_wet * (tracers + TIME_INCREMENT * (horizontal + vertical + reacted))


def ocean_update(padded, wetness, thermal_forcing_rate):
    height = padded.shape[2] - 4
    breadth = padded.shape[3] - 4

    def shifted(source, row_step, col_step):
        return source[:, :, 2 + row_step:height + 2 + row_step, 2 + col_step:breadth + 2 + col_step]

    central_entry = shifted(padded, 0, 0)
    wet_centre = shifted(wetness, 0, 0)
    neighbours = ((0, 1), (0, -1), (1, 0), (-1, 0))
    diffusive_curvature = jnp.zeros_like(central_entry)
    for row_step, col_step in neighbours:
        diffusive_curvature = diffusive_curvature + shifted(wetness, row_step, col_step) * (shifted(padded, row_step, col_step) - central_entry)
    diffusive_curvature = wet_centre * diffusive_curvature
    density = CONTRACTION * padded[3:4] - EXPANSION * padded[2:3]
    rho_centre = shifted(density, 0, 0)
    east_grad = 0.5 * (shifted(wetness, 0, 1) * (shifted(density, 0, 1) - rho_centre) + shifted(wetness, 0, -1) * (rho_centre - shifted(density, 0, -1)))
    north_grad = 0.5 * (shifted(wetness, 1, 0) * (shifted(density, 1, 0) - rho_centre) + shifted(wetness, -1, 0) * (rho_centre - shifted(density, -1, 0)))
    east_flow = central_entry[0]
    meridional = central_entry[1]
    seawater_warmth = central_entry[2]
    salinity = central_entry[3]
    energy = central_entry[4]
    grid_point_is_wet = wet_centre[0]
    level_open = grid_point_is_wet[1:] * grid_point_is_wet[:-1]
    sheared = ((east_flow[1:] - east_flow[:-1]) ** 2 + (meridional[1:] - meridional[:-1]) ** 2) * level_open
    sheared = jnp.concatenate([sheared, jnp.zeros_like(sheared[:1])], axis=0)
    fresh_zonal_speed = grid_point_is_wet * (east_flow + TIME_INCREMENT * (CORIOLIS * meridional - PRESSURE * east_grad[0] + VISCOSITY * diffusive_curvature[0] - DRAG_RATE * east_flow))
    fresh_poleward_speed = grid_point_is_wet * (meridional + TIME_INCREMENT * (-CORIOLIS * east_flow - PRESSURE * north_grad[0] + VISCOSITY * diffusive_curvature[1] - DRAG_RATE * meridional))
    fresh_thermal_state = grid_point_is_wet * (seawater_warmth + TIME_INCREMENT * (DIFFUSION_RATE * diffusive_curvature[2] + THERMAL_FORCING * thermal_forcing_rate))
    fresh_saltiness = grid_point_is_wet * (salinity + TIME_INCREMENT * (DIFFUSION_RATE * diffusive_curvature[3]))
    fresh_kinetic_budget = grid_point_is_wet * (energy + TIME_INCREMENT * (SHEAR_GAIN * sheared - DISSIPATION * energy))
    return jnp.stack([fresh_zonal_speed, fresh_poleward_speed, fresh_thermal_state, fresh_saltiness, fresh_kinetic_budget])


def reference(fields, sea_mask, bottom, reaction, growth):
    ocean_state = fields[0].reshape(FIELDS, 3, NZ, N_GY, TY, NX).transpose(0, 2, 3, 1, 4, 5).reshape(FIELDS, NZ, NY, NX)
    even_rows = (jnp.arange(N_GY) % 2 == 0)[None, None, None, :, None, None]
    groups = fields[1:].reshape(3, TRACERS, NZ, N_GY, TY, NX)
    ordered = jnp.where(even_rows, groups, groups[::-1])
    tracers = ordered.transpose(1, 2, 3, 0, 4, 5).reshape(TRACERS, NZ, NY, NX)
    levels = jnp.arange(NZ)[:, None, None]
    wet_cells = (sea_mask[None, :, :] * (levels < bottom[None, :, :])).astype(jnp.float32)
    wetness = jnp.pad(wet_cells, ((0, 0), (2, 2), (2, 2)))[None]
    margin = ((0, 0), (0, 0), (2, 2), (2, 2))
    for step_index in range(STEPS):
        kappas = KAPPA_BASE + KAPPA_GAIN * ocean_state[4]
        flow_pad = jnp.pad(jnp.stack([ocean_state[0], ocean_state[1], kappas]), margin)
        sunlight, thermal_forcing_rate = shading(tracers)
        next_ocean = ocean_update(jnp.pad(ocean_state, margin), wetness, thermal_forcing_rate)
        tracers = tracer_update(jnp.pad(tracers, margin), flow_pad[0:1], flow_pad[1:2], flow_pad[2:3], wetness, sunlight, reaction, growth)
        ocean_state = next_ocean
    ocean_slab = ocean_state.reshape(FIELDS, NZ, N_GY, 3, TY, NX).transpose(0, 3, 1, 2, 4, 5).reshape(TRACERS, NZ, N_GY * TY, NX)
    blocks = tracers.reshape(TRACERS, NZ, N_GY, 3, TY, NX).transpose(3, 0, 1, 2, 4, 5)
    tracer_slabs = jnp.where(even_rows, blocks, blocks[::-1]).reshape(3, TRACERS, NZ, N_GY * TY, NX)
    return jnp.concatenate([ocean_slab[None], tracer_slabs], axis=0)
```

```python
import functools

import jax
import jax.numpy as jnp
from jax import lax
from jax.experimental import pallas as pl
from jax.experimental.pallas import tpu as pltpu
from jax.sharding import PartitionSpec as P

STEPS = 2

TIME_INCREMENT = 0.2
CORIOLIS = 0.5
PRESSURE = 0.5
VISCOSITY = 0.15
DRAG_RATE = 0.1
DIFFUSION_RATE = 0.15
THERMAL_FORCING = 3.0
SHEAR_GAIN = 0.5
DISSIPATION = 0.5
KAPPA_BASE = 0.05
KAPPA_GAIN = 0.15
EXPANSION = 0.2
CONTRACTION = 0.8
WATER_SHADE = 0.05
CHLOROPHYLL_SHADE = 0.1
HALF_SAT = 0.5

MESH = pl.DeviceIdType.MESH
LANES = 128
SUBS = 8
KB = 4
SLOT_FIELD = (0, 1, 4, 2, 3)
U, V, E, T, S = range(5)


def minmod(a, b):
    return jnp.minimum(jnp.maximum(a, jnp.minimum(b, 0.0)), jnp.maximum(b, 0.0))


def iota(shape, dim):
    return lax.broadcasted_iota(jnp.int32, shape, dim)


def ahead(x, axis):
    return pltpu.roll(x, x.shape[axis] - 1, axis)


def behind(x, axis):
    return pltpu.roll(x, 1, axis)


def kernel(
    row_tiles, col_tiles,
    fields, depth, reaction, growth, out,
    state, base, coef_c, coef_r, coef_v, uptake, sun,
    col_out, col_in, row_out, row_in, orow_out, orow_in,
    flow_in, fcol_in, frow_in, heat_out, heat_in,
    send_sem, recv_sem,
):
    channels, levels, rows, cols = fields.shape[1:]
    section = lax.axis_index("section")
    g = lax.axis_index("gy")
    x = lax.axis_index("gx")
    is_ocean = section == 0
    is_tracer = section != 0
    even = lax.rem(g, 2) == 0
    third = jnp.maximum(jnp.where(even, section - 1, 3 - section), 0)
    band = 3 * g + third
    bands = 3 * row_tiles
    wide = cols + LANES

    def band_device(b):
        tile = b // 3
        t = lax.rem(b, 3)
        return (jnp.where(lax.rem(tile, 2) == 0, t + 1, 3 - t), tile, x)

    def own_tracer(t, col):
        return (jnp.where(even, t + 1, 3 - t), g, col)

    has_w, has_e = x > 0, x < col_tiles - 1
    has_s, has_n = g > 0, g < row_tiles - 1
    pairs = [(has_w, (section, g, x - 1)), (has_e, (section, g, x + 1))]
    pairs += [(is_ocean & has_s, (0, g - 1, x)), (is_ocean & has_n, (0, g + 1, x))]
    for t in range(3):
        pairs.append((is_ocean, own_tracer(t, x)))
        pairs.append((is_ocean & has_w, own_tracer(t, x - 1)))
        pairs.append((is_ocean & has_e, own_tracer(t, x + 1)))
    pairs.append((is_ocean & has_s, band_device(jnp.maximum(3 * g - 1, 0))))
    pairs.append((is_ocean & has_n, band_device(3 * g + 3)))
    has_lo, has_hi = band > 0, band < bands - 1
    pairs.append((is_tracer & has_lo, band_device(jnp.maximum(band - 1, 0))))
    pairs.append((is_tracer & has_hi, band_device(band + 1)))
    pairs.append((is_tracer, (0, g, x)))
    pairs.append((is_tracer & has_w, (0, g, x - 1)))
    pairs.append((is_tracer & has_e, (0, g, x + 1)))
    pairs.append((is_tracer & has_s & (third == 0), (0, g - 1, x)))
    pairs.append((is_tracer & has_n & (third == 2), (0, g + 1, x)))
    barrier = pltpu.get_barrier_semaphore()
    count = jnp.int32(0)
    for there, device in pairs:
        @pl.when(there)
        def _(device=device):
            pl.semaphore_signal(barrier, inc=1, device_id=device, device_id_type=MESH)
        count = count + there.astype(jnp.int32)

    def copy(src, dst, step, sent, received, device):
        return pltpu.make_async_remote_copy(
            src_ref=src, dst_ref=dst, send_sem=send_sem.at[step, sent],
            recv_sem=recv_sem.at[step, received], device_id=device, device_id_type=MESH,
        )

    def common_sends(step):
        return [
            (has_w, copy(col_out.at[step, 0], col_in.at[step, 1], step, 0, 1, (section, g, x - 1))),
            (has_e, copy(col_out.at[step, 1], col_in.at[step, 0], step, 1, 0, (section, g, x + 1))),
        ]

    def tracer_row_sends(step):
        return [
            (has_lo, copy(row_out.at[step, 0], row_in.at[step, 1], step, 2, 3, band_device(jnp.maximum(band - 1, 0)))),
            (has_hi, copy(row_out.at[step, 1], row_in.at[step, 0], step, 3, 2, band_device(band + 1))),
        ]

    def heat_send(step):
        return copy(heat_out.at[step], heat_in.at[step, third], step, 4, 9 + third, (0, g, x))

    def flow_sends(step):
        return [
            (is_ocean, copy(state.at[step, pl.ds(5 * t, 3), pl.ds(1, levels)], flow_in.at[step], step, 5 + t, 4, own_tracer(t, x)))
            for t in range(3)
        ]

    def ocean_edge_sends(step):
        found = []
        for t in range(3):
            cols_of = pl.ds(5 * t, 5)
            found.append((has_w, copy(col_out.at[step, 0, cols_of], fcol_in.at[step, 1], step, 8 + t, 6, own_tracer(t, x - 1))))
            found.append((has_e, copy(col_out.at[step, 1, cols_of], fcol_in.at[step, 0], step, 11 + t, 5, own_tracer(t, x + 1))))
            mine = 3 * g + t
            found.append((mine > 0, copy(orow_out.at[step, 0, pl.ds(5 * t + V, 2)], frow_in.at[step, 1], step, 14 + t, 8, band_device(jnp.maximum(mine - 1, 0)))))
            found.append((mine < bands - 1, copy(orow_out.at[step, 1, pl.ds(5 * t + V, 2)], frow_in.at[step, 0], step, 17 + t, 7, band_device(mine + 1))))
        found.append((has_s, copy(orow_out.at[step, 0, pl.ds(0, 5)], orow_in.at[step, 1], step, 2, 3, (0, g - 1, x))))
        found.append((has_n, copy(orow_out.at[step, 1, pl.ds(10, 5)], orow_in.at[step, 0], step, 3, 2, (0, g + 1, x))))
        return found

    def start(sends):
        for there, one in sends:
            @pl.when(there)
            def _(one=one):
                one.start()

    def finish(sends):
        for there, one in sends:
            @pl.when(there)
            def _(one=one):
                one.wait_send()

    def arrived(there, dst, step, received):
        @pl.when(there)
        def _():
            copy(dst, dst, step, 0, received, (section, g, x)).wait_recv()

    lane = iota((rows, LANES), 1)
    sub_full = iota((SUBS, cols), 0)
    for step in range(STEPS):
        for side, there in ((0, has_w), (1, has_e)):
            @pl.when(jnp.logical_not(there))
            def _(step=step, side=side):
                col_in[step, side] = jnp.zeros(col_in.shape[2:], jnp.float32)
                fcol_in[step, side] = jnp.zeros(fcol_in.shape[2:], jnp.float32)
        for side, there, ocean_there in ((0, has_lo, has_s), (1, has_hi, has_n)):
            @pl.when(is_tracer & jnp.logical_not(there))
            def _(step=step, side=side):
                row_in[step, side] = jnp.zeros(row_in.shape[2:], jnp.float32)
                frow_in[step, side] = jnp.zeros(frow_in.shape[2:], jnp.float32)
            @pl.when(is_ocean & jnp.logical_not(ocean_there))
            def _(step=step, side=side):
                orow_in[step, side] = jnp.zeros(orow_in.shape[2:], jnp.float32)

    def pack_columns(step):
        def one(c, carry):
            low = jnp.zeros((rows, LANES), jnp.float32)
            high = low
            for k in range(levels):
                mine = (lane >= 2 * k) & (lane < 2 * k + 2)
                left = state[step, c, k + 1, :, :LANES]
                right = state[step, c, k + 1, :, cols - LANES:]
                if k:
                    left = pltpu.roll(left, 2 * k, 1)
                low = jnp.where(mine, left, low)
                high = jnp.where(mine, pltpu.roll(right, (2 * k + 2) % LANES, 1), high)
            col_out[step, 0, c] = low
            col_out[step, 1, c] = high
            return carry
        lax.fori_loop(0, channels, one, 0)

    def column_halo(low, high, k):
        east = high if k == 0 else pltpu.roll(high, LANES - 2 * k, 1)
        west = pltpu.roll(low, (LANES - 2 - 2 * k) % LANES, 1)
        return jnp.where(lane < LANES // 2, east, west)

    def widen(value, low, high, k):
        return jnp.concatenate([value, column_halo(low, high, k)], axis=-1)

    def depth_views(t):
        base_row = pl.multiple_of(rows + rows * t, rows)
        row = pl.ds(base_row, rows)
        middle = depth[row, LANES:LANES + cols]
        halo = jnp.where(lane < LANES // 2, depth[row, LANES + cols:], depth[row, :LANES])
        across = jnp.concatenate([middle, halo], axis=-1)
        above = depth[pl.ds(pl.multiple_of(base_row + rows, rows), rows), LANES:LANES + cols]
        below = depth[pl.ds(pl.multiple_of(base_row - rows, rows), rows), LANES:LANES + cols]
        along = jnp.concatenate([middle, jnp.where(sub_full < SUBS // 2, above, below)], axis=0)
        return middle, across, along

    def tracer():
        middle, across, along = depth_views(third)
        across_next = ahead(across, 1)
        along_next = ahead(along, 0)
        both_c = jnp.minimum(across, across_next)
        both_r = jnp.minimum(along, along_next)

        def load(c, carry):
            state[0, c, pl.ds(1, levels)] = fields[0, c]
            for slot in range(2):
                state[slot, c, 0] = jnp.zeros((rows, cols), jnp.float32)
                state[slot, c, levels + 1] = jnp.zeros((rows, cols), jnp.float32)
            return carry
        lax.fori_loop(0, channels, load, 0)

        for step in range(STEPS):
            last = step == STEPS - 1

            def pack_rows(c, carry):
                for k in range(levels):
                    row_out[step, 0, c, 2 * k:2 * k + 2] = state[step, c, k + 1, 0:2]
                    row_out[step, 1, c, 2 * k:2 * k + 2] = state[step, c, k + 1, rows - 2:rows]
                return carry
            lax.fori_loop(0, channels, pack_rows, 0)
            if step == 0:
                pl.semaphore_wait(barrier, count)
            start(tracer_row_sends(step))
            optical = jnp.zeros((rows, cols), jnp.float32)
            for k in range(levels):
                chlorophyll = jnp.maximum(state[step, 2, k + 1], 0.0)
                light = jnp.exp(-optical)
                heat_out[step, k] = CHLOROPHYLL_SHADE * chlorophyll * light
                optical = optical + (WATER_SHADE + CHLOROPHYLL_SHADE * chlorophyll)
                nutrient = jnp.maximum(state[step, 0, k + 1], 0.0)
                uptake[k] = nutrient / (nutrient + HALF_SAT) * light * TIME_INCREMENT
            heat_send(step).start()
            pack_columns(step)
            start(common_sends(step))

            def react(k, carry):
                values = [state[step, c, k + 1] for c in range(channels)]
                growing = [
                    growth[d] * (jnp.maximum(values[d], 0.0) * uptake[k]) for d in range(channels)
                ]
                for c in range(channels):
                    total = values[c]
                    for d in range(channels):
                        total = total + reaction[c, d] * growing[d]
                    base[c, k] = total
                return carry
            lax.fori_loop(0, levels, react, 0)

            arrived(is_tracer, flow_in.at[step], step, 4)
            arrived(has_w, fcol_in.at[step, 0], step, 5)
            arrived(has_e, fcol_in.at[step, 1], step, 6)
            arrived(has_lo, frow_in.at[step, 0], step, 7)
            arrived(has_hi, frow_in.at[step, 1], step, 8)
            zero = jnp.zeros((rows, cols), jnp.float32)
            coef_v[0] = zero
            coef_v[levels] = zero
            for k in range(levels):
                speed = widen(flow_in[step, U, k], fcol_in[step, 0, U], fcol_in[step, 1, U], k)
                kappa = KAPPA_BASE + KAPPA_GAIN * widen(
                    flow_in[step, E, k], fcol_in[step, 0, E], fcol_in[step, 1, E], k
                )
                opened = jnp.where(k < both_c, TIME_INCREMENT, 0.0)
                flow = speed * opened
                coef_c[0, k] = jnp.maximum(flow, 0.0)
                coef_c[1, k] = jnp.minimum(flow, 0.0)
                coef_c[2, k] = 0.5 * (kappa + ahead(kappa, 1)) * opened
                low_v = jnp.broadcast_to(frow_in[step, 0, 0, k:k + 1], (rows, cols))
                low_e = jnp.broadcast_to(frow_in[step, 0, 1, k:k + 1], (rows, cols))
                high_e = jnp.broadcast_to(frow_in[step, 1, 1, k:k + 1], (rows, cols))
                speed = jnp.concatenate([flow_in[step, V, k], low_v], axis=0)
                kappa = KAPPA_BASE + KAPPA_GAIN * jnp.concatenate(
                    [flow_in[step, E, k], jnp.where(sub_full < SUBS // 2, high_e, low_e)], axis=0
                )
                opened = jnp.where(k < both_r, TIME_INCREMENT, 0.0)
                flow = speed * opened
                coef_r[0, k] = jnp.maximum(flow, 0.0)
                coef_r[1, k] = jnp.minimum(flow, 0.0)
                coef_r[2, k] = 0.5 * (kappa + ahead(kappa, 0)) * opened
                if k:
                    mean = KAPPA_BASE + 0.5 * KAPPA_GAIN * (flow_in[step, E, k - 1] + flow_in[step, E, k])
                    coef_v[k] = mean * jnp.where(k < middle, TIME_INCREMENT, 0.0)

            arrived(has_w, col_in.at[step, 0], step, 0)
            arrived(has_e, col_in.at[step, 1], step, 1)
            arrived(has_lo, row_in.at[step, 0], step, 2)
            arrived(has_hi, row_in.at[step, 1], step, 3)

            def fluxes(q, coefs, k0, axis):
                window = pl.ds(k0, KB)
                change = ahead(q, axis) - q
                half = 0.5 * minmod(change, behind(change, axis))
                flux = (
                    coefs[0, window] * (q + half)
                    + coefs[1, window] * ahead(q - half, axis)
                    - coefs[2, window] * change
                )
                return behind(flux, axis) - flux

            def advance(c, carry):
                low_c, high_c = col_in[step, 0, c], col_in[step, 1, c]
                for k0 in range(0, levels, KB):
                    q = state[step, c, pl.ds(k0 + 1, KB)]
                    halo = jnp.stack([column_halo(low_c, high_c, k0 + j) for j in range(KB)])
                    total = base[c, pl.ds(k0, KB)]
                    total = total + fluxes(jnp.concatenate([q, halo], axis=2), coef_c, k0, 2)[:, :, :cols]
                    low_r = row_in[step, 0, c, pl.ds(2 * k0, 2 * KB)]
                    high_r = row_in[step, 1, c, pl.ds(2 * k0, 2 * KB)]
                    halo = jnp.stack([
                        jnp.where(
                            sub_full < SUBS // 2,
                            pltpu.roll(high_r, SUBS - 2 * j, 0) if j else high_r,
                            pltpu.roll(low_r, SUBS - 2 - 2 * j, 0) if j < KB - 1 else low_r,
                        )
                        for j in range(KB)
                    ])
                    total = total + fluxes(jnp.concatenate([q, halo], axis=1), coef_r, k0, 1)[:, :rows]
                    up = coef_v[pl.ds(k0 + 1, KB)] * (state[step, c, pl.ds(k0 + 2, KB)] - q)
                    down = coef_v[pl.ds(k0, KB)] * (q - state[step, c, pl.ds(k0, KB)])
                    total = total + (up - down)
                    fresh = jnp.stack([
                        jnp.where(k0 + j < middle, total[j], 0.0) for j in range(KB)
                    ])
                    if last:
                        out[0, c, pl.ds(k0, KB)] = fresh
                    else:
                        state[step + 1, c, pl.ds(k0 + 1, KB)] = fresh
                return carry
            lax.fori_loop(0, channels, advance, 0)

        for step in range(STEPS):
            finish(tracer_row_sends(step) + common_sends(step))
            heat_send(step).wait_send()

    def ocean():
        def load(t, carry):
            for slot in range(5):
                state[0, 5 * t + slot, pl.ds(1, levels)] = fields[0, 3 * SLOT_FIELD[slot] + t]
                for step in range(2):
                    state[step, 5 * t + slot, levels + 1] = jnp.zeros((rows, cols), jnp.float32)
            return carry
        lax.fori_loop(0, 3, load, 0)
        views = []
        for t in range(3):
            middle, across, along = depth_views(t)
            views.append((
                middle,
                ahead(across, 1)[:, :cols], behind(across, 1)[:, :cols],
                ahead(along, 0)[:rows], behind(along, 0)[:rows],
            ))

        for step in range(STEPS):
            last = step == STEPS - 1
            if step == 0:
                pl.semaphore_wait(barrier, count)
                start(flow_sends(step))

            def pack_rows(c, carry):
                for k in range(levels):
                    orow_out[step, 0, c, k:k + 1] = state[step, c, k + 1, 0:1]
                    orow_out[step, 1, c, k:k + 1] = state[step, c, k + 1, rows - 1:rows]
                return carry
            lax.fori_loop(0, channels, pack_rows, 0)
            pack_columns(step)
            start(ocean_edge_sends(step))
            start(common_sends(step))
            arrived(has_w, col_in.at[step, 0], step, 0)
            arrived(has_e, col_in.at[step, 1], step, 1)
            arrived(has_s, orow_in.at[step, 0], step, 2)
            arrived(has_n, orow_in.at[step, 1], step, 3)

            def store(t, slot, k, value):
                if last:
                    out[0, 3 * SLOT_FIELD[slot] + t, k] = value
                else:
                    state[step + 1, 5 * t + slot, k + 1] = value

            def level(k, carry):
                for t in range(3):
                    middle, east_d, west_d, north_d, south_d = views[t]
                    m = [
                        jnp.where(k < d, 1.0, 0.0)
                        for d in (middle, east_d, west_d, north_d, south_d)
                    ]
                    centre, steps = {}, {}
                    for slot in (U, V, T, S):
                        c = 5 * t + slot
                        value = state[step, c, k + 1]
                        low, high = col_in[step, 0, c], col_in[step, 1, c]
                        east = pltpu.roll(high, lax.rem(LANES - 2 * k, LANES), 1)
                        west = pltpu.roll(low, lax.rem(2 * LANES - 2 - 2 * k, LANES), 1)
                        ext = jnp.concatenate(
                            [value, jnp.where(lane < LANES // 2, east, west)], axis=-1
                        )
                        if t == 2:
                            top = orow_in[step, 1, slot, pl.ds(k, 1)]
                        else:
                            top = state[step, c + 5, k + 1, 0:1]
                        if t == 0:
                            bottom_row = orow_in[step, 0, slot, pl.ds(k, 1)]
                        else:
                            bottom_row = state[step, c - 5, k + 1, rows - 1:rows]
                        north = jnp.where(
                            sub_full == rows - 1, jnp.broadcast_to(top, (rows, cols)), ahead(value, 0)
                        )
                        south = jnp.where(
                            sub_full == 0, jnp.broadcast_to(bottom_row, (rows, cols)), behind(value, 0)
                        )
                        centre[slot] = value
                        steps[slot] = [
                            m[1] * (ahead(ext, 1)[:, :cols] - value),
                            m[2] * (behind(ext, 1)[:, :cols] - value),
                            m[3] * (north - value),
                            m[4] * (south - value),
                        ]
                    lap = {s: (v[0] + v[1] + v[2] + v[3]) * m[0] for s, v in steps.items()}
                    rho = [CONTRACTION * a - EXPANSION * b for a, b in zip(steps[S], steps[T])]
                    grad_x = 0.5 * (rho[0] - rho[1])
                    grad_y = 0.5 * (rho[2] - rho[3])
                    u, v = centre[U], centre[V]
                    energy = state[step, 5 * t + E, k + 1]
                    du = state[step, 5 * t + U, k + 2] - u
                    dv = state[step, 5 * t + V, k + 2] - v
                    shear = jnp.where(k + 1 < middle, du * du + dv * dv, 0.0)
                    store(t, U, k, m[0] * (u + TIME_INCREMENT * (
                        CORIOLIS * v - PRESSURE * grad_x + VISCOSITY * lap[U] - DRAG_RATE * u)))
                    store(t, V, k, m[0] * (v + TIME_INCREMENT * (
                        -CORIOLIS * u - PRESSURE * grad_y + VISCOSITY * lap[V] - DRAG_RATE * v)))
                    store(t, E, k, m[0] * (energy + TIME_INCREMENT * (
                        SHEAR_GAIN * shear - DISSIPATION * energy)))
                    store(t, T, k, m[0] * (centre[T] + TIME_INCREMENT * DIFFUSION_RATE * lap[T]))
                    store(t, S, k, m[0] * (centre[S] + TIME_INCREMENT * DIFFUSION_RATE * lap[S]))
                return carry
            lax.fori_loop(0, levels, level, 0)
            if not last:
                start(flow_sends(step + 1))
            for t in range(3):
                arrived(is_ocean, heat_in.at[step, t], step, 9 + t)

            def warm(k, carry):
                for t in range(3):
                    heat = jnp.where(
                        k < views[t][0], TIME_INCREMENT * THERMAL_FORCING * heat_in[step, t, k], 0.0
                    )
                    if last:
                        out[0, 3 * SLOT_FIELD[T] + t, k] = out[0, 3 * SLOT_FIELD[T] + t, k] + heat
                    else:
                        state[step + 1, 5 * t + T, k + 1] = state[step + 1, 5 * t + T, k + 1] + heat
                return carry
            lax.fori_loop(0, levels, warm, 0)

        for step in range(STEPS):
            finish(flow_sends(step) + ocean_edge_sends(step) + common_sends(step))

    pl.when(is_tracer)(tracer)
    pl.when(is_ocean)(ocean)


def on_device(fields, sea_mask, bottom, reaction, growth):
    _, channels, levels, rows, cols = fields.shape
    row_tiles, col_tiles = lax.axis_size("gy"), lax.axis_size("gx")
    depth = jnp.where(sea_mask == 1, bottom, 0)
    depth = jnp.pad(depth, ((rows, rows), (LANES, LANES)))
    depth = lax.dynamic_slice(
        depth,
        (lax.axis_index("gy") * 3 * rows, lax.axis_index("gx") * cols),
        (5 * rows, cols + 2 * LANES),
    )
    f32 = jnp.float32
    vmem = pl.BlockSpec(memory_space=pltpu.VMEM)
    smem = pl.BlockSpec(memory_space=pltpu.SMEM)
    return pl.pallas_call(
        functools.partial(kernel, row_tiles, col_tiles),
        out_shape=jax.ShapeDtypeStruct(fields.shape, f32),
        in_specs=[vmem, vmem, smem, smem],
        out_specs=vmem,
        scratch_shapes=[
            pltpu.VMEM((2, channels, levels + 2, rows, cols), f32),
            pltpu.VMEM((channels, levels, rows, cols), f32),
            pltpu.VMEM((3, levels, rows, cols + LANES), f32),
            pltpu.VMEM((3, levels, 2 * rows, cols), f32),
            pltpu.VMEM((levels + 1, rows, cols), f32),
            pltpu.VMEM((levels, rows, cols), f32),
            pltpu.VMEM((levels, rows, cols), f32),
            pltpu.VMEM((2, 2, channels, rows, LANES), f32),
            pltpu.VMEM((2, 2, channels, rows, LANES), f32),
            pltpu.VMEM((2, 2, channels, 2 * levels, cols), f32),
            pltpu.VMEM((2, 2, channels, 2 * levels, cols), f32),
            pltpu.VMEM((2, 2, channels, levels, cols), f32),
            pltpu.VMEM((2, 2, 5, levels, cols), f32),
            pltpu.VMEM((2, 3, levels, rows, cols), f32),
            pltpu.VMEM((2, 2, 5, rows, LANES), f32),
            pltpu.VMEM((2, 2, 2, levels, cols), f32),
            pltpu.VMEM((2, levels, rows, cols), f32),
            pltpu.VMEM((2, 3, levels, rows, cols), f32),
            pltpu.SemaphoreType.DMA((2, 20)),
            pltpu.SemaphoreType.DMA((2, 12)),
        ],
        compiler_params=pltpu.CompilerParams(
            collective_id=0, has_side_effects=True, vmem_limit_bytes=48 * 1024 * 1024
        ),
    )(fields, depth, reaction, growth)


def solution(mesh):
    return jax.shard_map(
        on_device,
        mesh=mesh,
        in_specs=(P("section", None, None, "gy", "gx"), P(), P(), P(), P()),
        out_specs=P("section", None, None, "gy", "gx"),
        check_vma=False,
    )
```

```python
import functools

import jax
import jax.numpy as jnp
from jax import lax
from jax.experimental import pallas as pl
from jax.experimental.pallas import tpu as pltpu
from jax.sharding import PartitionSpec as P

STEPS = 2

TIME_INCREMENT = 0.2
CORIOLIS = 0.5
PRESSURE = 0.5
VISCOSITY = 0.15
DRAG_RATE = 0.1
DIFFUSION_RATE = 0.15
THERMAL_FORCING = 3.0
SHEAR_GAIN = 0.5
DISSIPATION = 0.5
KAPPA_BASE = 0.05
KAPPA_GAIN = 0.15
EXPANSION = 0.2
CONTRACTION = 0.8
WATER_SHADE = 0.05
CHLOROPHYLL_SHADE = 0.1
HALF_SAT = 0.5

MESH = pl.DeviceIdType.MESH
LANES = 128
SUBS = 8
KB = 2
SLOT_FIELD = (0, 1, 4, 2, 3)
U, V, E, T, S = range(5)


def minmod(a, b):
    return jnp.minimum(jnp.maximum(a, jnp.minimum(b, 0.0)), jnp.maximum(b, 0.0))


def iota(shape, dim):
    return lax.broadcasted_iota(jnp.int32, shape, dim)


def ahead(x, axis):
    return pltpu.roll(x, x.shape[axis] - 1, axis)


def turned(x, shift):
    shift %= SUBS
    return pltpu.roll(x, shift, 0) if shift else x


def behind(x, axis):
    return pltpu.roll(x, 1, axis)


def kernel(
    row_tiles, col_tiles,
    fields, depth, reaction_hbm, growth_hbm, out,
    state, base, coef_c, coef_r, coef_v, uptake, sun,
    col_out, col_in, row_out, row_in, orow_out, orow_in,
    flow_in, fcol_in, frow_in, heat_out, heat_in,
    send_sem, recv_sem, load_sem, reaction, growth,
):
    channels, levels, rows, cols = fields.shape[1:]
    section = lax.axis_index("section")
    g = lax.axis_index("gy")
    x = lax.axis_index("gx")
    is_ocean = section == 0
    is_tracer = section != 0
    even = lax.rem(g, 2) == 0
    third = jnp.maximum(jnp.where(even, section - 1, 3 - section), 0)
    band = 3 * g + third
    bands = 3 * row_tiles
    wide = cols + LANES

    def band_device(b):
        tile = b // 3
        t = lax.rem(b, 3)
        return (jnp.where(lax.rem(tile, 2) == 0, t + 1, 3 - t), tile, x)

    def own_tracer(t, col):
        return (jnp.where(even, t + 1, 3 - t), g, col)

    has_w, has_e = x > 0, x < col_tiles - 1
    has_s, has_n = g > 0, g < row_tiles - 1
    pairs = [(has_w, (section, g, x - 1)), (has_e, (section, g, x + 1))]
    pairs += [(is_ocean & has_s, (0, g - 1, x)), (is_ocean & has_n, (0, g + 1, x))]
    for t in range(3):
        pairs.append((is_ocean, own_tracer(t, x)))
        pairs.append((is_ocean & has_w, own_tracer(t, x - 1)))
        pairs.append((is_ocean & has_e, own_tracer(t, x + 1)))
    pairs.append((is_ocean & has_s, band_device(jnp.maximum(3 * g - 1, 0))))
    pairs.append((is_ocean & has_n, band_device(3 * g + 3)))
    has_lo, has_hi = band > 0, band < bands - 1
    pairs.append((is_tracer & has_lo, band_device(jnp.maximum(band - 1, 0))))
    pairs.append((is_tracer & has_hi, band_device(band + 1)))
    pairs.append((is_tracer, (0, g, x)))
    pairs.append((is_tracer & has_w, (0, g, x - 1)))
    pairs.append((is_tracer & has_e, (0, g, x + 1)))
    pairs.append((is_tracer & has_s & (third == 0), (0, g - 1, x)))
    pairs.append((is_tracer & has_n & (third == 2), (0, g + 1, x)))
    barrier = pltpu.get_barrier_semaphore()
    count = jnp.int32(0)
    for there, device in pairs:
        @pl.when(there)
        def _(device=device):
            pl.semaphore_signal(barrier, inc=1, device_id=device, device_id_type=MESH)
        count = count + there.astype(jnp.int32)

    def copy(src, dst, step, sent, received, device):
        return pltpu.make_async_remote_copy(
            src_ref=src, dst_ref=dst, send_sem=send_sem.at[step, sent],
            recv_sem=recv_sem.at[step, received], device_id=device, device_id_type=MESH,
        )

    def common_sends(step):
        return [
            (has_w, copy(col_out.at[step, 0], col_in.at[step, 1], step, 0, 1, (section, g, x - 1))),
            (has_e, copy(col_out.at[step, 1], col_in.at[step, 0], step, 1, 0, (section, g, x + 1))),
        ]

    part = channels // 3

    def tracer_row_sends(step, j):
        some = pl.ds(part * j, part)
        return [
            (has_lo, copy(row_out.at[step, 0, some], row_in.at[step, 1, some], step, 20 + j, 15 + j, band_device(jnp.maximum(band - 1, 0)))),
            (has_hi, copy(row_out.at[step, 1, some], row_in.at[step, 0, some], step, 23 + j, 12 + j, band_device(band + 1))),
        ]

    def heat_send(step):
        return copy(heat_out.at[step], heat_in.at[step, third], step, 4, 9 + third, (0, g, x))

    def sent(step):
        return 2 if step else 3

    def flow_sends(step):
        return [
            (is_ocean, copy(state.at[step, pl.ds(5 * t, sent(step)), pl.ds(1, levels)], flow_in.at[step, pl.ds(0, sent(step))], step, 5 + t, 4, own_tracer(t, x)))
            for t in range(3)
        ]

    def ocean_edge_sends(step):
        found = []
        for t in range(3):
            cols_of = pl.ds(5 * t, 5)
            found.append((has_w, copy(col_out.at[step, 0, cols_of], fcol_in.at[step, 1], step, 8 + t, 6, own_tracer(t, x - 1))))
            found.append((has_e, copy(col_out.at[step, 1, cols_of], fcol_in.at[step, 0], step, 11 + t, 5, own_tracer(t, x + 1))))
            mine = 3 * g + t
            found.append((mine > 0, copy(orow_out.at[step, 0, pl.ds(5 * t + V, 2)], frow_in.at[step, 1], step, 14 + t, 8, band_device(jnp.maximum(mine - 1, 0)))))
            found.append((mine < bands - 1, copy(orow_out.at[step, 1, pl.ds(5 * t + V, 2)], frow_in.at[step, 0], step, 17 + t, 7, band_device(mine + 1))))
        found.append((has_s, copy(orow_out.at[step, 0, pl.ds(0, 5)], orow_in.at[step, 1], step, 2, 3, (0, g - 1, x))))
        found.append((has_n, copy(orow_out.at[step, 1, pl.ds(10, 5)], orow_in.at[step, 0], step, 3, 2, (0, g + 1, x))))
        return found

    def start(sends):
        for there, one in sends:
            @pl.when(there)
            def _(one=one):
                one.start()

    def finish(sends):
        for there, one in sends:
            @pl.when(there)
            def _(one=one):
                one.wait_send()

    def arrived(there, dst, step, received):
        @pl.when(there)
        def _():
            copy(dst, dst, step, 0, received, (section, g, x)).wait_recv()

    lane = iota((rows, LANES), 1)
    sub_full = iota((SUBS, cols), 0)
    for step in range(STEPS):
        for side, there in ((0, has_w), (1, has_e)):
            @pl.when(jnp.logical_not(there))
            def _(step=step, side=side):
                col_in[step, side] = jnp.zeros(col_in.shape[2:], jnp.float32)
                fcol_in[step, side] = jnp.zeros(fcol_in.shape[2:], jnp.float32)
        for side, there, ocean_there in ((0, has_lo, has_s), (1, has_hi, has_n)):
            @pl.when(is_tracer & jnp.logical_not(there))
            def _(step=step, side=side):
                row_in[step, side] = jnp.zeros(row_in.shape[2:], jnp.float32)
                frow_in[step, side] = jnp.zeros(frow_in.shape[2:], jnp.float32)
            @pl.when(is_ocean & jnp.logical_not(ocean_there))
            def _(step=step, side=side):
                orow_in[step, side] = jnp.zeros(orow_in.shape[2:], jnp.float32)

    def pack_columns(step):
        def one(c, carry):
            low = jnp.zeros((rows, LANES), jnp.float32)
            high = low
            for k in range(levels):
                mine = (lane >= 2 * k) & (lane < 2 * k + 2)
                left = state[step, c, k + 1, :, :LANES]
                right = state[step, c, k + 1, :, cols - LANES:]
                if k:
                    left = pltpu.roll(left, 2 * k, 1)
                low = jnp.where(mine, left, low)
                high = jnp.where(mine, pltpu.roll(right, (2 * k + 2) % LANES, 1), high)
            col_out[step, 0, c] = low
            col_out[step, 1, c] = high
            return carry
        lax.fori_loop(0, channels, one, 0)

    def column_halo(low, high, k):
        east = high if k == 0 else pltpu.roll(high, LANES - 2 * k, 1)
        west = pltpu.roll(low, (LANES - 2 - 2 * k) % LANES, 1)
        return jnp.where(lane < LANES // 2, east, west)

    def widen(value, low, high, k):
        return jnp.concatenate([value, column_halo(low, high, k)], axis=-1)

    def depth_views(t):
        base_row = pl.multiple_of(rows + rows * t, rows)
        row = pl.ds(base_row, rows)
        middle = depth[row, LANES:LANES + cols]
        halo = jnp.where(lane < LANES // 2, depth[row, LANES + cols:], depth[row, :LANES])
        across = jnp.concatenate([middle, halo], axis=-1)
        above = depth[pl.ds(pl.multiple_of(base_row + rows, rows), rows), LANES:LANES + cols]
        below = depth[pl.ds(pl.multiple_of(base_row - rows, rows), rows), LANES:LANES + cols]
        along = jnp.concatenate([middle, jnp.where(sub_full < SUBS // 2, above, below)], axis=0)
        return middle, across, along

    def tracer():
        middle, across, along = depth_views(third)
        across_next = ahead(across, 1)
        along_next = ahead(along, 0)
        both_c = jnp.minimum(across, across_next)
        both_r = jnp.minimum(along, along_next)

        def load(c, carry):
            for slot in range(2):
                state[slot, c, 0] = jnp.zeros((rows, cols), jnp.float32)
                state[slot, c, levels + 1] = jnp.zeros((rows, cols), jnp.float32)
            return carry
        whole = pltpu.make_async_copy(fields.at[0], state.at[0, :, pl.ds(1, levels)], load_sem.at[0])
        whole.start()
        tables = [
            pltpu.make_async_copy(reaction_hbm, reaction, load_sem.at[1]),
            pltpu.make_async_copy(growth_hbm, growth, load_sem.at[2]),
        ]
        for one in tables:
            one.start()
        lax.fori_loop(0, channels, load, 0)
        whole.wait()

        for step in range(STEPS):
            last = step == STEPS - 1

            def pack_rows(c, carry):
                for k in range(levels):
                    row_out[step, 0, c, 2 * k:2 * k + 2] = state[step, c, k + 1, 0:2]
                    row_out[step, 1, c, 2 * k:2 * k + 2] = state[step, c, k + 1, rows - 2:rows]
                return carry
            if step == 0:
                lax.fori_loop(0, channels, pack_rows, 0)
                pl.semaphore_wait(barrier, count)
                for j in range(3):
                    start(tracer_row_sends(step, j))
            pack_columns(step)
            start(common_sends(step))
            optical = jnp.zeros((rows, cols), jnp.float32)
            for k in range(levels):
                chlorophyll = jnp.maximum(state[step, 2, k + 1], 0.0)
                light = jnp.exp(-optical)
                heat_out[step, k] = CHLOROPHYLL_SHADE * chlorophyll * light
                optical = optical + (WATER_SHADE + CHLOROPHYLL_SHADE * chlorophyll)
                nutrient = jnp.maximum(state[step, 0, k + 1], 0.0)
                uptake[k] = nutrient / (nutrient + HALF_SAT) * light * TIME_INCREMENT
            heat_send(step).start()
            if step == 0:
                for one in tables:
                    one.wait()

            def react(k, carry):
                values = [state[step, c, k + 1] for c in range(channels)]
                growing = [
                    growth[d] * (jnp.maximum(values[d], 0.0) * uptake[k]) for d in range(channels)
                ]
                for c in range(channels):
                    total = values[c]
                    for d in range(channels):
                        total = total + reaction[c, d] * growing[d]
                    base[c, k] = total
                return carry
            lax.fori_loop(0, levels, react, 0)

            arrived(is_tracer, flow_in.at[step, pl.ds(0, sent(step))], step, 4)
            if step:
                for k in range(levels):
                    energy = flow_in[step - 1, E, k]
                    shear = jnp.zeros((rows, cols), jnp.float32)
                    if k < levels - 1:
                        du = flow_in[step - 1, U, k + 1] - flow_in[step - 1, U, k]
                        dv = flow_in[step - 1, V, k + 1] - flow_in[step - 1, V, k]
                        shear = jnp.where(k + 1 < middle, du * du + dv * dv, 0.0)
                    flow_in[step, E, k] = jnp.where(k < middle, energy + TIME_INCREMENT * (
                        SHEAR_GAIN * shear - DISSIPATION * energy), 0.0)
            arrived(has_w, fcol_in.at[step, 0], step, 5)
            arrived(has_e, fcol_in.at[step, 1], step, 6)
            arrived(has_lo, frow_in.at[step, 0], step, 7)
            arrived(has_hi, frow_in.at[step, 1], step, 8)
            zero = jnp.zeros((rows, cols), jnp.float32)
            coef_v[0] = zero
            coef_v[levels] = zero
            for k in range(levels):
                speed = widen(flow_in[step, U, k], fcol_in[step, 0, U], fcol_in[step, 1, U], k)
                kappa = KAPPA_BASE + KAPPA_GAIN * widen(
                    flow_in[step, E, k], fcol_in[step, 0, E], fcol_in[step, 1, E], k
                )
                opened = jnp.where(k < both_c, TIME_INCREMENT, 0.0)
                flow = speed * opened
                coef_c[0, k] = jnp.maximum(flow, 0.0)
                coef_c[1, k] = jnp.minimum(flow, 0.0)
                coef_c[2, k] = 0.5 * (kappa + ahead(kappa, 1)) * opened
                low_v = jnp.broadcast_to(frow_in[step, 0, 0, k:k + 1], (rows, cols))
                low_e = jnp.broadcast_to(frow_in[step, 0, 1, k:k + 1], (rows, cols))
                high_e = jnp.broadcast_to(frow_in[step, 1, 1, k:k + 1], (rows, cols))
                speed = jnp.concatenate([flow_in[step, V, k], low_v], axis=0)
                kappa = KAPPA_BASE + KAPPA_GAIN * jnp.concatenate(
                    [flow_in[step, E, k], jnp.where(sub_full < SUBS // 2, high_e, low_e)], axis=0
                )
                opened = jnp.where(k < both_r, TIME_INCREMENT, 0.0)
                flow = speed * opened
                coef_r[0, k] = jnp.maximum(flow, 0.0)
                coef_r[1, k] = jnp.minimum(flow, 0.0)
                coef_r[2, k] = 0.5 * (kappa + ahead(kappa, 0)) * opened
                if k:
                    mean = KAPPA_BASE + 0.5 * KAPPA_GAIN * (flow_in[step, E, k - 1] + flow_in[step, E, k])
                    coef_v[k] = mean * jnp.where(k < middle, TIME_INCREMENT, 0.0)

            arrived(has_w, col_in.at[step, 0], step, 0)
            arrived(has_e, col_in.at[step, 1], step, 1)

            def fluxes(q, coefs, k0, axis):
                window = pl.ds(k0, KB)
                change = ahead(q, axis) - q
                half = 0.5 * minmod(change, behind(change, axis))
                flux = (
                    coefs[0, window] * (q + half)
                    + coefs[1, window] * ahead(q - half, axis)
                    - coefs[2, window] * change
                )
                return behind(flux, axis) - flux

            def advance_columns(c, carry):
                low_c, high_c = col_in[step, 0, c], col_in[step, 1, c]
                for k0 in range(0, levels, KB):
                    q = state[step, c, pl.ds(k0 + 1, KB)]
                    halo = jnp.stack([column_halo(low_c, high_c, k0 + j) for j in range(KB)])
                    total = base[c, pl.ds(k0, KB)]
                    total = total + fluxes(jnp.concatenate([q, halo], axis=2), coef_c, k0, 2)[:, :, :cols]
                    up = coef_v[pl.ds(k0 + 1, KB)] * (state[step, c, pl.ds(k0 + 2, KB)] - q)
                    down = coef_v[pl.ds(k0, KB)] * (q - state[step, c, pl.ds(k0, KB)])
                    base[c, pl.ds(k0, KB)] = total + (up - down)
                return carry
            lax.fori_loop(0, channels, advance_columns, 0)

            def advance_rows(c, carry):
                for k0 in range(0, levels, KB):
                    q = state[step, c, pl.ds(k0 + 1, KB)]
                    total = base[c, pl.ds(k0, KB)]
                    first = 2 * k0 % SUBS
                    low_r = row_in[step, 0, c, pl.ds(2 * k0 - first, SUBS)]
                    high_r = row_in[step, 1, c, pl.ds(2 * k0 - first, SUBS)]
                    halo = jnp.stack([
                        jnp.where(
                            sub_full < SUBS // 2,
                            turned(high_r, -first - 2 * j),
                            turned(low_r, -2 - first - 2 * j),
                        )
                        for j in range(KB)
                    ])
                    total = total + fluxes(jnp.concatenate([q, halo], axis=1), coef_r, k0, 1)[:, :rows]
                    fresh = jnp.stack([
                        jnp.where(k0 + j < middle, total[j], 0.0) for j in range(KB)
                    ])
                    if last:
                        out[0, c, pl.ds(k0, KB)] = fresh
                    else:
                        state[step + 1, c, pl.ds(k0 + 1, KB)] = fresh
                        for j in range(KB):
                            two = slice(2 * (k0 + j), 2 * (k0 + j) + 2)
                            row_out[step + 1, 0, c, two] = fresh[j, 0:2]
                            row_out[step + 1, 1, c, two] = fresh[j, rows - 2:rows]
                return carry
            for j in range(3):
                some = pl.ds(part * j, part)
                arrived(has_lo, row_in.at[step, 0, some], step, 12 + j)
                arrived(has_hi, row_in.at[step, 1, some], step, 15 + j)
                lax.fori_loop(part * j, part * (j + 1), advance_rows, 0)
                if not last:
                    start(tracer_row_sends(step + 1, j))

        for step in range(STEPS):
            finish(common_sends(step))
            for j in range(3):
                finish(tracer_row_sends(step, j))
            heat_send(step).wait_send()

    def ocean():
        loads = [
            pltpu.make_async_copy(
                fields.at[0, 3 * SLOT_FIELD[slot] + t],
                state.at[0, 5 * t + slot, pl.ds(1, levels)],
                load_sem.at[5 * t + slot],
            )
            for t in range(3) for slot in range(5)
        ]
        for one in loads:
            one.start()

        def load(t, carry):
            for slot in range(5):
                for step in range(2):
                    state[step, 5 * t + slot, levels + 1] = jnp.zeros((rows, cols), jnp.float32)
            return carry
        lax.fori_loop(0, 3, load, 0)
        for one in loads:
            one.wait()
        views = []
        for t in range(3):
            middle, across, along = depth_views(t)
            views.append((
                middle,
                ahead(across, 1)[:, :cols], behind(across, 1)[:, :cols],
                ahead(along, 0)[:rows], behind(along, 0)[:rows],
            ))

        for step in range(STEPS):
            last = step == STEPS - 1
            if step == 0:
                pl.semaphore_wait(barrier, count)
                start(flow_sends(step))

            def pack_rows(c, carry):
                for k in range(levels):
                    orow_out[step, 0, c, k:k + 1] = state[step, c, k + 1, 0:1]
                    orow_out[step, 1, c, k:k + 1] = state[step, c, k + 1, rows - 1:rows]
                return carry
            lax.fori_loop(0, channels, pack_rows, 0)
            pack_columns(step)
            start(ocean_edge_sends(step))
            start(common_sends(step))
            arrived(has_w, col_in.at[step, 0], step, 0)
            arrived(has_e, col_in.at[step, 1], step, 1)
            arrived(has_s, orow_in.at[step, 0], step, 2)
            arrived(has_n, orow_in.at[step, 1], step, 3)

            def store(t, slot, k, value):
                if last:
                    out[0, 3 * SLOT_FIELD[slot] + t, k] = value
                else:
                    state[step + 1, 5 * t + slot, k + 1] = value

            def level(k, carry):
                for t in range(3):
                    middle, east_d, west_d, north_d, south_d = views[t]
                    m = [
                        jnp.where(k < d, 1.0, 0.0)
                        for d in (middle, east_d, west_d, north_d, south_d)
                    ]
                    centre, steps = {}, {}
                    for slot in (U, V, T, S):
                        c = 5 * t + slot
                        value = state[step, c, k + 1]
                        low, high = col_in[step, 0, c], col_in[step, 1, c]
                        east = pltpu.roll(high, lax.rem(LANES - 2 * k, LANES), 1)
                        west = pltpu.roll(low, lax.rem(2 * LANES - 2 - 2 * k, LANES), 1)
                        ext = jnp.concatenate(
                            [value, jnp.where(lane < LANES // 2, east, west)], axis=-1
                        )
                        if t == 2:
                            top = orow_in[step, 1, slot, pl.ds(k, 1)]
                        else:
                            top = state[step, c + 5, k + 1, 0:1]
                        if t == 0:
                            bottom_row = orow_in[step, 0, slot, pl.ds(k, 1)]
                        else:
                            bottom_row = state[step, c - 5, k + 1, rows - 1:rows]
                        north = jnp.where(
                            sub_full == rows - 1, jnp.broadcast_to(top, (rows, cols)), ahead(value, 0)
                        )
                        south = jnp.where(
                            sub_full == 0, jnp.broadcast_to(bottom_row, (rows, cols)), behind(value, 0)
                        )
                        centre[slot] = value
                        steps[slot] = [
                            m[1] * (ahead(ext, 1)[:, :cols] - value),
                            m[2] * (behind(ext, 1)[:, :cols] - value),
                            m[3] * (north - value),
                            m[4] * (south - value),
                        ]
                    lap = {s: (v[0] + v[1] + v[2] + v[3]) * m[0] for s, v in steps.items()}
                    rho = [CONTRACTION * a - EXPANSION * b for a, b in zip(steps[S], steps[T])]
                    grad_x = 0.5 * (rho[0] - rho[1])
                    grad_y = 0.5 * (rho[2] - rho[3])
                    u, v = centre[U], centre[V]
                    energy = state[step, 5 * t + E, k + 1]
                    du = state[step, 5 * t + U, k + 2] - u
                    dv = state[step, 5 * t + V, k + 2] - v
                    shear = jnp.where(k + 1 < middle, du * du + dv * dv, 0.0)
                    store(t, U, k, m[0] * (u + TIME_INCREMENT * (
                        CORIOLIS * v - PRESSURE * grad_x + VISCOSITY * lap[U] - DRAG_RATE * u)))
                    store(t, V, k, m[0] * (v + TIME_INCREMENT * (
                        -CORIOLIS * u - PRESSURE * grad_y + VISCOSITY * lap[V] - DRAG_RATE * v)))
                    store(t, E, k, m[0] * (energy + TIME_INCREMENT * (
                        SHEAR_GAIN * shear - DISSIPATION * energy)))
                    store(t, T, k, m[0] * (centre[T] + TIME_INCREMENT * DIFFUSION_RATE * lap[T]))
                    store(t, S, k, m[0] * (centre[S] + TIME_INCREMENT * DIFFUSION_RATE * lap[S]))
                return carry
            lax.fori_loop(0, levels, level, 0)
            if not last:
                start(flow_sends(step + 1))
            for t in range(3):
                arrived(is_ocean, heat_in.at[step, t], step, 9 + t)

            def warm(k, carry):
                for t in range(3):
                    heat = jnp.where(
                        k < views[t][0], TIME_INCREMENT * THERMAL_FORCING * heat_in[step, t, k], 0.0
                    )
                    if last:
                        out[0, 3 * SLOT_FIELD[T] + t, k] = out[0, 3 * SLOT_FIELD[T] + t, k] + heat
                    else:
                        state[step + 1, 5 * t + T, k + 1] = state[step + 1, 5 * t + T, k + 1] + heat
                return carry
            lax.fori_loop(0, levels, warm, 0)

        for step in range(STEPS):
            finish(flow_sends(step) + ocean_edge_sends(step) + common_sends(step))

    pl.when(is_tracer)(tracer)
    pl.when(is_ocean)(ocean)


def on_device(fields, sea_mask, bottom, reaction, growth):
    _, channels, levels, rows, cols = fields.shape
    row_tiles, col_tiles = lax.axis_size("gy"), lax.axis_size("gx")
    depth = jnp.where(sea_mask == 1, bottom, 0)
    depth = jnp.pad(depth, ((rows, rows), (LANES, LANES)))
    depth = lax.dynamic_slice(
        depth,
        (lax.axis_index("gy") * 3 * rows, lax.axis_index("gx") * cols),
        (5 * rows, cols + 2 * LANES),
    )
    f32 = jnp.float32
    vmem = pl.BlockSpec(memory_space=pltpu.VMEM)
    whole = pl.BlockSpec(memory_space=pltpu.HBM)
    return pl.pallas_call(
        functools.partial(kernel, row_tiles, col_tiles),
        out_shape=jax.ShapeDtypeStruct(fields.shape, f32),
        in_specs=[whole, vmem, whole, whole],
        out_specs=vmem,
        scratch_shapes=[
            pltpu.VMEM((2, channels, levels + 2, rows, cols), f32),
            pltpu.VMEM((channels, levels, rows, cols), f32),
            pltpu.VMEM((3, levels, rows, cols + LANES), f32),
            pltpu.VMEM((3, levels, 2 * rows, cols), f32),
            pltpu.VMEM((levels + 1, rows, cols), f32),
            pltpu.VMEM((levels, rows, cols), f32),
            pltpu.VMEM((levels, rows, cols), f32),
            pltpu.VMEM((2, 2, channels, rows, LANES), f32),
            pltpu.VMEM((2, 2, channels, rows, LANES), f32),
            pltpu.VMEM((2, 2, channels, 2 * levels, cols), f32),
            pltpu.VMEM((2, 2, channels, 2 * levels, cols), f32),
            pltpu.VMEM((2, 2, channels, levels, cols), f32),
            pltpu.VMEM((2, 2, 5, levels, cols), f32),
            pltpu.VMEM((2, 3, levels, rows, cols), f32),
            pltpu.VMEM((2, 2, 5, rows, LANES), f32),
            pltpu.VMEM((2, 2, 2, levels, cols), f32),
            pltpu.VMEM((2, levels, rows, cols), f32),
            pltpu.VMEM((2, 3, levels, rows, cols), f32),
            pltpu.SemaphoreType.DMA((2, 26)),
            pltpu.SemaphoreType.DMA((2, 18)),
            pltpu.SemaphoreType.DMA((15,)),
            pltpu.SMEM(reaction.shape, f32),
            pltpu.SMEM(growth.shape, f32),
        ],
        compiler_params=pltpu.CompilerParams(
            collective_id=0, has_side_effects=True, vmem_limit_bytes=48 * 1024 * 1024
        ),
    )(fields, depth, reaction, growth)


def solution(mesh):
    return jax.shard_map(
        on_device,
        mesh=mesh,
        in_specs=(P("section", None, None, "gy", "gx"), P(), P(), P(), P()),
        out_specs=P("section", None, None, "gy", "gx"),
        check_vma=False,
    )
```
